32 devices in a mesh: groups: 2 (over y), dp: 4 (over x, core), tensor: 4 (over z).
Axes of the slice: x: 2, y: 2, z: 4, core: 2. Of those that a mesh axis runs over, the one named last changes fastest.
Arguments:
- tokens: bfloat16 [8192, 8192], P(('groups', 'dp'), 'tensor'), parts along dimension 0, may hold values from -6 to 6
- key_value_weight: bfloat16 [8192, 2048], P('tensor'), may hold values from -0.0625 to 0.0625
- adapter_down_factors: bfloat16 [48, 8192, 64], P(('groups', 'dp'), 'tensor'), parts along dimension 0, may hold values from -0.0625 to 0.0625
- adapter_up_factors: bfloat16 [48, 64, 2048], P(('groups', 'dp'), None, 'tensor'), parts along dimension 0, may hold values from -0.375 to 0.375
- adapter_per_block: int32 [64], P('groups'), parts along dimension 0, may hold values from 0 to 23, as said below
- live_rows_per_block: int32 [64], P(('groups', 'dp')), parts along dimension 0, may hold values from 1 to 128, as said below
- adapter_storage_slot: int32 [48], P('groups'), parts along dimension 0, may hold values from 0 to 23, each once
Outputs:
- keys_values: bfloat16 [8192, 2048], P(('groups', 'dp'), 'tensor'), parts along dimension 0
The draws below stay inside these ranges and needn't reach their ends.
There are 2 independent parts, one for each index of `groups`. The reference program is written for one: setup_inputs(seed, part) draws one part's arguments, and reference() takes and returns one part's arrays. A program takes and returns all parts, laid end to end along the dimension named above; an argument that names none is the same for every part. Nothing has to cross between parts.
Inputs may be any that keep to these rules, and one draw needn't show every extreme that they name: `adapter_per_block`: the blocks of one adapter stand together; one adapter holds exactly 6 blocks, every other used one 1 to 3; about half as many adapters as blocks are used. `live_rows_per_block`: every block of an adapter is full but its last one.
All inputs are finite; a program needn't handle non-finite values.
Results may differ from the reference program's by a relative error of at most 0.001.
Values may be sent and summed in bfloat16 or wider, within the bound.
A program may use at most 128 MiB of HBM per device.

```python
import jax
import jax.numpy as jnp
from jax import lax

MODEL_WIDTH = 8192
KEY_VALUE_WIDTH = 2048
ADAPTER_RANK = 64
BLK = 128
NBLOCKS = 32
TOKENS = 4096
ADAPTER_COUNT = 24


def blocks_plan(key):
    used = NBLOCKS // 2 - 2
    others = used - 1
    key_coin, key_order, key_ids, key_live = jax.random.split(key, 4)
    pairs = max(others // 2, 1)
    coins = jax.random.randint(key_coin, (pairs,), 0, 2)
    places = jnp.arange(others)
    pair_index = jnp.minimum(places // 2, pairs - 1)
    paired = places // 2 < others // 2
    signs = jnp.where(places % 2 == 0, 1, -1)
    extra = jnp.where(paired, signs * coins[pair_index], 0)
    lengths = jnp.concatenate([jnp.array([6], jnp.int32), (2 + extra).astype(jnp.int32)])
    order = jax.random.permutation(key_order, used)
    lengths = lengths[order]
    ends = jnp.cumsum(lengths)
    block_ids = jnp.arange(NBLOCKS)
    segment = jnp.sum((block_ids[:, None] >= ends[None, :]).astype(jnp.int32), axis=1)
    chosen_ids = jax.random.permutation(key_ids, ADAPTER_COUNT)[:used]
    adapters = chosen_ids[segment]
    live_last = jax.random.randint(key_live, (used,), 1, BLK + 1)
    is_last = block_ids == ends[segment] - 1
    live_rows = jnp.where(is_last, live_last[segment], BLK)
    return (adapters.astype(jnp.int32), live_rows.astype(jnp.int32))


def draw_adapter_per_block(key, part):
    adapters, live_rows = blocks_plan(key)
    return adapters


def draw_live_rows_per_block(key, part):
    adapters, live_rows = blocks_plan(key)
    return live_rows


def shard_levels(own_key, shape, shards, least, largest):
    gain = 1.0
    for dim, parts in shards:
        draws = jax.random.uniform(jax.random.fold_in(jax.random.fold_in(own_key, 6), dim), (parts,), jnp.float32, least / len(shards), largest / len(shards))
        gain = gain * jnp.repeat(jnp.exp(draws), shape[dim] // parts).reshape((-1,) + (1,) * (len(shape) - 1 - dim))
    return gain


def bell_draw(stream_key, shape, scale, reach, cuts=(), held_as=jnp.bfloat16):
    gain = shard_levels(stream_key, shape, cuts, -0.22, 0.18) if cuts else 1.0
    values = jax.random.normal(stream_key, shape, jnp.float32) * scale * gain
    return jnp.minimum(jnp.maximum(values, -reach), reach).astype(held_as)


def setup_inputs(seed: int = 0, part: int = 0) -> dict:
    splits = jax.random.split(jax.random.key(seed), 8)
    own_keys = jax.random.split(jax.random.fold_in(splits[7], part), 8)
    return {
        "tokens": bell_draw(own_keys[0], (TOKENS, MODEL_WIDTH), 1.0, 6.0, ((0, 4), (1, 4))),
        "key_value_weight": bell_draw(splits[1], (MODEL_WIDTH, KEY_VALUE_WIDTH), MODEL_WIDTH ** -0.5, 0.0625, ((0, 4),)),
        "adapter_down_factors": bell_draw(own_keys[2], (ADAPTER_COUNT, MODEL_WIDTH, ADAPTER_RANK), MODEL_WIDTH ** -0.5, 0.0625, ((0, 4), (1, 4))),
        "adapter_up_factors": bell_draw(own_keys[3], (ADAPTER_COUNT, ADAPTER_RANK, KEY_VALUE_WIDTH), (4 * ADAPTER_RANK) ** -0.5, 0.375, ((0, 4), (2, 4))),
        "adapter_per_block": draw_adapter_per_block(jax.random.fold_in(jax.random.fold_in(splits[7], part), 71), part),
        "live_rows_per_block": draw_live_rows_per_block(jax.random.fold_in(jax.random.fold_in(splits[7], part), 71), part),
        "adapter_storage_slot": jax.random.permutation(own_keys[6], ADAPTER_COUNT).astype(jnp.int32),
    }


ADAPTER_SCALE = 2.0


def reference(tokens, key_value_weight, adapter_down_factors, adapter_up_factors, adapter_per_block, live_rows_per_block, adapter_storage_slot):
    block_count = adapter_per_block.shape[0]
    block_length = tokens.shape[0] // block_count
    base_output = jnp.dot(tokens, key_value_weight, preferred_element_type=jnp.float32)
    storage_slots = adapter_storage_slot[adapter_per_block].astype(jnp.int32)

    def single_block(operands):
        tokens_in_block, current_slot = operands
        lowrank_output = jnp.dot(tokens_in_block, adapter_down_factors[current_slot], preferred_element_type=jnp.float32)
        return jnp.dot(lowrank_output, adapter_up_factors[current_slot].astype(jnp.float32), precision=lax.Precision.HIGHEST)

    adapter_term = lax.map(single_block, (tokens.reshape(block_count, block_length, tokens.shape[1]), storage_slots))
    combined_output = base_output.reshape(block_count, block_length, -1) + ADAPTER_SCALE * adapter_term
    live_rows = jnp.arange(block_length, dtype=jnp.int32)[None, :] < live_rows_per_block[:, None]
    result = jnp.where(live_rows[:, :, None], combined_output, jnp.float32(0.0))
    return result.reshape(tokens.shape[0], -1).astype(jnp.bfloat16)
```

```python
import functools

import jax
import jax.numpy as jnp
from jax import lax
from jax.experimental import pallas as pl
from jax.experimental.pallas import tpu as pltpu
from jax.sharding import PartitionSpec as P

ADAPTER_SCALE = 2.0
MESH = pl.DeviceIdType.MESH
F32 = jnp.float32
LEVELS = 32767.0


def kernel(
    T, X, R, NB, BL,
    apb, slot_of, live, tok_h, w_h, dn_h, up_h, out,
    tok, w, dn, up, acc, low,
    su, sd, ru, rd, ssu, ssd, rsu, rsd,
    lsu, lsd, lru, lrd,
    sem_tok, sem_w, sem_own,
    s_u, s_d, r_u, r_d, s_us, s_ds, r_us, r_ds,
    s_low, r_low, s_x, r_x, s_c, r_c,
):
    RB = tok.shape[0] // R
    AP = dn_h.shape[0]
    t = lax.axis_index("tensor")
    pos = lax.axis_index("dp")
    x, core = pos // 2, pos % 2
    right = lax.rem(x + 1, X) * 2 + core
    left = lax.rem(x + X - 1, X) * 2 + core
    partner = x * 2 + 1 - core
    has_lo, has_hi = t > 0, t < T - 1

    def rows(r):
        return pl.ds(pl.multiple_of(r * RB, RB), RB)

    N = w_h.shape[1] // T
    order = []
    for p in range((T + 1) // 2):
        for d in (T - 1 - p, p):
            if d not in order:
                order.append(d)

    def w_copy(d):
        return pltpu.make_async_copy(w_h.at[:, d * N:(d + 1) * N], w.at[d], sem_w.at[d])

    def tok_copy(r):
        return pltpu.make_async_copy(tok_h.at[rows(r)], tok.at[rows(r)], sem_tok.at[r])

    w_copy(order[0]).start()
    tok_copy(0).start()
    w_copy(order[1]).start()
    for r in range(1, R):
        tok_copy(r).start()
    for d in order[2:]:
        w_copy(d).start()

    def piece(ref, owner):
        return ref.at[pl.ds(owner * AP, AP)]

    own_dn = pltpu.make_async_copy(dn_h, piece(dn, pos), sem_own.at[0])
    own_up = pltpu.make_async_copy(up_h, piece(up, pos), sem_own.at[1])
    own_dn.start()
    own_up.start()

    bar = pltpu.get_barrier_semaphore()

    @pl.when(has_lo)
    def _():
        pl.semaphore_signal(bar, inc=1, device_id={"tensor": t - 1}, device_id_type=MESH)

    @pl.when(has_hi)
    def _():
        pl.semaphore_signal(bar, inc=1, device_id={"tensor": t + 1}, device_id_type=MESH)

    peers = [partner]
    if X > 1:
        peers.append(right)
    if X > 2:
        peers.append(left)
    for q in peers:
        pl.semaphore_signal(bar, inc=1, device_id={"dp": q}, device_id_type=MESH)
    pl.semaphore_wait(bar, has_lo.astype(jnp.int32) + has_hi.astype(jnp.int32) + len(peers))

    def x_copy(s, k):
        owner = lax.rem(x - s + X, X) * 2 + core
        full, mine = (dn, dn_h) if k == 0 else (up, up_h)
        return pltpu.make_async_remote_copy(
            src_ref=mine if s == 0 else piece(full, owner), dst_ref=piece(full, owner),
            send_sem=s_x.at[s, k], recv_sem=r_x.at[s, k],
            device_id={"dp": right}, device_id_type=MESH)

    def c_copy(s, k):
        owner = lax.rem(x - s + X, X) * 2 + core
        full, mine = (dn, dn_h) if k == 0 else (up, up_h)
        return pltpu.make_async_remote_copy(
            src_ref=mine if s == 0 else piece(full, owner), dst_ref=piece(full, owner),
            send_sem=s_c.at[s, k], recv_sem=r_c.at[s, k],
            device_id={"dp": partner}, device_id_type=MESH)

    if X > 1:
        for k in range(2):
            x_copy(0, k).start()
    for k in range(2):
        c_copy(0, k).start()

    def u_copy(i, r):
        return (
            pltpu.make_async_remote_copy(
                src_ref=su.at[i, rows(r)], dst_ref=ru.at[i, rows(r)], send_sem=s_u.at[i, r],
                recv_sem=r_u.at[i, r], device_id={"tensor": t + 1}, device_id_type=MESH),
            pltpu.make_async_remote_copy(
                src_ref=ssu.at[i, r], dst_ref=rsu.at[i, r], send_sem=s_us.at[i, r],
                recv_sem=r_us.at[i, r], device_id={"tensor": t + 1}, device_id_type=MESH),
        )

    def d_copy(i, r):
        return (
            pltpu.make_async_remote_copy(
                src_ref=sd.at[i, rows(r)], dst_ref=rd.at[i, rows(r)], send_sem=s_d.at[i, r],
                recv_sem=r_d.at[i, r], device_id={"tensor": t - 1}, device_id_type=MESH),
            pltpu.make_async_remote_copy(
                src_ref=ssd.at[i, r], dst_ref=rsd.at[i, r], send_sem=s_ds.at[i, r],
                recv_sem=r_ds.at[i, r], device_id={"tensor": t - 1}, device_id_type=MESH),
        )

    def product(d, r):
        return jnp.dot(tok[rows(r), :], w[d], preferred_element_type=F32)

    def encode(v, q_ref, s_ref, i, r):
        top = jnp.maximum(jnp.max(jnp.abs(v), axis=0, keepdims=True), 1e-30)
        q_ref[i, rows(r), :] = jnp.round(v * (LEVELS / top)).astype(jnp.int32).astype(jnp.int16)
        s_ref[i, r] = top * (1.0 / LEVELS)

    def decode(q_ref, s_ref, i, r):
        return q_ref[i, rows(r), :].astype(jnp.int32).astype(F32) * s_ref[i, r]

    def phase(p):
        du, dd = T - 1 - p, p
        iu, idn = du - 1, dd

        def chunk(r, _):
            if p == 0:
                tok_copy(r).wait()

            @pl.when(t < du)
            def _():
                acc[rows(r), :] = product(du, r)

                @pl.when(has_lo)
                def _():
                    for c in u_copy(iu, r):
                        c.wait_recv()
                    acc[rows(r), :] += decode(ru, rsu, iu, r)

                encode(acc[rows(r), :], su, ssu, iu, r)
                for c in u_copy(iu, r):
                    c.start()

            if p == 0:
                @pl.when(r == 0)
                def _():
                    if order[1] != order[0]:
                        w_copy(order[1]).wait()

            @pl.when(t > dd)
            def _():
                acc[rows(r), :] = product(dd, r)

                @pl.when(has_hi)
                def _():
                    for c in d_copy(idn, r):
                        c.wait_recv()
                    acc[rows(r), :] += decode(rd, rsd, idn, r)

                encode(acc[rows(r), :], sd, ssd, idn, r)
                for c in d_copy(idn, r):
                    c.start()

            return 0

        lax.fori_loop(0, R, chunk, 0)

    def low_start():
        own_dn.wait()
        own_up.wait()
        for s in range(X - 1):
            for k in range(2):
                x_copy(s, k).wait_recv()
            for k in range(2):
                if s < X - 2:
                    x_copy(s + 1, k).start()
                c_copy(s + 1, k).start()
        for s in range(X):
            for k in range(2):
                c_copy(s, k).wait_recv()

        def block(b, _):
            slot = slot_of[apb[pos * NB + b]]
            at = pl.ds(pl.multiple_of(b * BL, BL), BL)
            low[b] = lax.dot_general(
                dn[slot], tok[at, :], (((1,), (1,)), ((), ())), preferred_element_type=F32)
            return 0

        lax.fori_loop(0, NB, block, 0)

        @pl.when(t == 0)
        def _():
            lsu[...] = low[...]
            low_up().start()

        @pl.when(t == T - 1)
        def _():
            lsd[...] = low[...]
            low_down().start()

    def low_up():
        return pltpu.make_async_remote_copy(
            src_ref=lsu, dst_ref=lru, send_sem=s_low.at[0], recv_sem=r_low.at[0],
            device_id={"tensor": t + 1}, device_id_type=MESH)

    def low_down():
        return pltpu.make_async_remote_copy(
            src_ref=lsd, dst_ref=lrd, send_sem=s_low.at[1], recv_sem=r_low.at[1],
            device_id={"tensor": t - 1}, device_id_type=MESH)

    def low_finish():
        @pl.when(has_lo)
        def _():
            low_up().wait_recv()

            @pl.when(has_hi)
            def _():
                lsu[...] = low[...] + lru[...]
                low_up().start()

        @pl.when(has_hi)
        def _():
            low_down().wait_recv()

            @pl.when(has_lo)
            def _():
                lsd[...] = low[...] + lrd[...]
                low_down().start()

            low[...] += lrd[...]

        @pl.when(has_lo)
        def _():
            low[...] += lru[...]

    waited = {order[0]}
    w_copy(order[0]).wait()
    for p in range(T - 1):
        if p == 0:
            waited.add(order[1])
        else:
            for d in (T - 1 - p, p):
                if d not in waited:
                    w_copy(d).wait()
                    waited.add(d)
        if p == T - 2:
            low_start()
        phase(p)

    def own(r, _):
        acc[rows(r), :] = product(t, r)
        return 0

    lax.fori_loop(0, R, own, 0)
    low_finish()

    def lora(b, _):
        slot = slot_of[apb[pos * NB + b]]
        at = pl.ds(pl.multiple_of(b * BL, BL), BL)
        whole = low[b]
        first = whole.astype(jnp.bfloat16)
        rest = whole - first.astype(F32)
        second = rest.astype(jnp.bfloat16)
        third = (rest - second.astype(F32)).astype(jnp.bfloat16)
        factor = up[slot]
        term = lax.dot_general(
            jnp.concatenate([first, second, third], axis=0),
            jnp.concatenate([factor] * 3, axis=0),
            (((0,), (0,)), ((), ())), preferred_element_type=F32)
        acc[at, :] += ADAPTER_SCALE * term
        return 0

    lax.fori_loop(0, NB, lora, 0)

    def finish(r, _):
        @pl.when(has_hi)
        def _():
            for c in d_copy(t, r):
                c.wait_recv()
            acc[rows(r), :] += decode(rd, rsd, t, r)

        @pl.when(has_lo)
        def _():
            for c in u_copy(t - 1, r):
                c.wait_recv()
            acc[rows(r), :] += decode(ru, rsu, t - 1, r)

        for j in range(RB // BL):
            b = r * (RB // BL) + j
            at = pl.ds(pl.multiple_of(b * BL, BL), BL)
            here = lax.broadcasted_iota(jnp.int32, (BL, N), 0) < live[b]
            out[at, :] = jnp.where(here, acc[at, :], 0.0).astype(out.dtype)
        return 0

    lax.fori_loop(0, R, finish, 0)

    for p in range(T - 1):
        du, dd = T - 1 - p, p

        def sent(r, _):
            @pl.when(t < du)
            def _():
                for c in u_copy(du - 1, r):
                    c.wait_send()

            @pl.when(t > dd)
            def _():
                for c in d_copy(dd, r):
                    c.wait_send()

            return 0

        lax.fori_loop(0, R, sent, 0)

    @pl.when(has_hi)
    def _():
        low_up().wait_send()

    @pl.when(has_lo)
    def _():
        low_down().wait_send()

    for k in range(2):
        for s in range(X - 1):
            x_copy(s, k).wait_send()
        for s in range(X):
            c_copy(s, k).wait_send()


def on_device(T, DP, tokens, weight, down, up, apb, live, slot_of):
    X = DP // 2
    M, K = tokens.shape
    N = weight.shape[1] // T
    NB = live.shape[0]
    BL = M // NB
    AP, RANK = down.shape[0], down.shape[2]
    A = AP * DP
    R = max(1, min(4, NB))
    down = jnp.swapaxes(down, 1, 2)
    bf16, i16 = jnp.bfloat16, jnp.int16
    D = max(T - 1, 1)
    V, DMA = pltpu.VMEM, pltpu.SemaphoreType.DMA
    smem = pl.BlockSpec(memory_space=pltpu.SMEM)
    hbm = pl.BlockSpec(memory_space=pl.ANY)
    scratch = (
        [V((M, K), bf16), V((T, K, N), bf16), V((A, RANK, K), bf16), V((A, RANK, N), bf16)]
        + [V((M, N), F32), V((NB, RANK, BL), F32)]
        + [V((D, M, N), i16)] * 4
        + [V((D, R, 1, N), F32)] * 4
        + [V((NB, RANK, BL), F32)] * 4
        + [DMA((R,)), DMA((T,)), DMA((2,))]
        + [DMA((D, R))] * 8
        + [DMA((2,)), DMA((2,))]
        + [DMA((max(X - 1, 1), 2)), DMA((max(X - 1, 1), 2)), DMA((X, 2)), DMA((X, 2))]
    )
    return pl.pallas_call(
        functools.partial(kernel, T, X, R, NB, BL),
        out_shape=jax.ShapeDtypeStruct((M, N), bf16),
        in_specs=[smem, smem, smem, hbm, hbm, hbm, hbm],
        out_specs=pl.BlockSpec(memory_space=pltpu.VMEM),
        scratch_shapes=scratch,
        compiler_params=pltpu.CompilerParams(
            collective_id=0, has_side_effects=True, vmem_limit_bytes=56 * 2**20),
        cost_estimate=pl.CostEstimate(
            flops=2 * M * K * N * T, bytes_accessed=2 * (M * K + K * N * T), transcendentals=0),
    )(apb, slot_of, live, tokens, weight, down, up)


def solution(mesh):
    placed = (
        P(("groups", "dp"), "tensor"),
        P("tensor", None),
        P(("groups", "dp"), "tensor", None),
        P(("groups", "dp"), None, "tensor"),
        P("groups"),
        P(("groups", "dp")),
        P("groups"),
    )
    return jax.shard_map(
        functools.partial(on_device, mesh.shape["tensor"], mesh.shape["dp"]),
        mesh=mesh,
        in_specs=placed,
        out_specs=P(("groups", "dp"), "tensor"),
        check_vma=False,
    )
```

```python
import functools

import jax
import jax.numpy as jnp
from jax import lax
from jax.experimental import pallas as pl
from jax.experimental.pallas import tpu as pltpu
from jax.sharding import PartitionSpec as P

ADAPTER_SCALE = 2.0
MESH = pl.DeviceIdType.MESH
F32 = jnp.float32
LEVELS = 32767.0
AHEAD = 2
LAG = 2


def kernel(
    T, X, R, NB, BL,
    apb, slot_of, live, tok_h, w_h, dn_h, up_h, out,
    tok, w, dn, up, acc, hold, low,
    su, sd, ru, rd, ssu, ssd, rsu, rsd,
    lsu, lsd, lru, lrd, slu, sld, rlu, rld,
    sem_tok, sem_w, sem_own,
    s_u, s_d, r_u, r_d, s_us, s_ds, r_us, r_ds,
    s_low, r_low, s_x, r_x, s_c, r_c,
):
    RB = tok.shape[0] // R
    AP = dn_h.shape[0]
    t = lax.axis_index("tensor")
    pos = lax.axis_index("dp")
    x, core = pos // 2, pos % 2
    right = lax.rem(x + 1, X) * 2 + core
    left = lax.rem(x + X - 1, X) * 2 + core
    partner = x * 2 + 1 - core
    has_lo, has_hi = t > 0, t < T - 1

    def rows(r):
        return pl.ds(pl.multiple_of(r * RB, RB), RB)

    N = w_h.shape[1] // T
    order = []
    for p in range((T + 1) // 2):
        for d in (T - 1 - p, p):
            if d not in order:
                order.append(d)

    def w_copy(d):
        return pltpu.make_async_copy(w_h.at[:, d * N:(d + 1) * N], w.at[d], sem_w.at[d])

    def tok_copy(r):
        return pltpu.make_async_copy(tok_h.at[rows(r)], tok.at[rows(r)], sem_tok.at[r])

    lower = t < T // 2
    upper = jnp.logical_not(lower)
    lag_u = LAG * upper.astype(jnp.int32)
    lag_d = LAG - lag_u

    @pl.when(lower)
    def _():
        w_copy(T - 1).start()

    @pl.when(upper)
    def _():
        w_copy(0).start()

    tok_copy(0).start()

    def load_rest():
        @pl.when(lower)
        def _():
            w_copy(0).start()

        @pl.when(upper)
        def _():
            w_copy(T - 1).start()

        for r in range(1, R):
            tok_copy(r).start()
        for d in order[2:]:
            w_copy(d).start()
        own_dn.start()
        own_up.start()

    def piece(ref, owner):
        return ref.at[pl.ds(owner * AP, AP)]

    own_dn = pltpu.make_async_copy(dn_h, piece(dn, pos), sem_own.at[0])
    own_up = pltpu.make_async_copy(up_h, piece(up, pos), sem_own.at[1])
    bar = pltpu.get_barrier_semaphore()

    @pl.when(has_lo)
    def _():
        pl.semaphore_signal(bar, inc=1, device_id={"tensor": t - 1}, device_id_type=MESH)

    @pl.when(has_hi)
    def _():
        pl.semaphore_signal(bar, inc=1, device_id={"tensor": t + 1}, device_id_type=MESH)

    peers = [partner]
    if X > 1:
        peers.append(right)
    if X > 2:
        peers.append(left)
    for q in peers:
        pl.semaphore_signal(bar, inc=1, device_id={"dp": q}, device_id_type=MESH)
    def x_copy(s, k):
        owner = lax.rem(x - s + X, X) * 2 + core
        full, mine = (dn, dn_h) if k == 0 else (up, up_h)
        return pltpu.make_async_remote_copy(
            src_ref=mine if s == 0 else piece(full, owner), dst_ref=piece(full, owner),
            send_sem=s_x.at[s, k], recv_sem=r_x.at[s, k],
            device_id={"dp": right}, device_id_type=MESH)

    def c_copy(s, k):
        owner = lax.rem(x - s + X, X) * 2 + core
        full, mine = (dn, dn_h) if k == 0 else (up, up_h)
        return pltpu.make_async_remote_copy(
            src_ref=mine if s == 0 else piece(full, owner), dst_ref=piece(full, owner),
            send_sem=s_c.at[s, k], recv_sem=r_c.at[s, k],
            device_id={"dp": partner}, device_id_type=MESH)

    def gather_start():
        if X > 1:
            for k in range(2):
                x_copy(0, k).start()
        for k in range(2):
            c_copy(0, k).start()

    def u_copy(i, r):
        return (
            pltpu.make_async_remote_copy(
                src_ref=su.at[i, rows(r)], dst_ref=ru.at[i, rows(r)], send_sem=s_u.at[i, r],
                recv_sem=r_u.at[i, r], device_id={"tensor": t + 1}, device_id_type=MESH),
            pltpu.make_async_remote_copy(
                src_ref=ssu.at[i, r], dst_ref=rsu.at[i, r], send_sem=s_us.at[i, r],
                recv_sem=r_us.at[i, r], device_id={"tensor": t + 1}, device_id_type=MESH),
        )

    def d_copy(i, r):
        return (
            pltpu.make_async_remote_copy(
                src_ref=sd.at[i, rows(r)], dst_ref=rd.at[i, rows(r)], send_sem=s_d.at[i, r],
                recv_sem=r_d.at[i, r], device_id={"tensor": t - 1}, device_id_type=MESH),
            pltpu.make_async_remote_copy(
                src_ref=ssd.at[i, r], dst_ref=rsd.at[i, r], send_sem=s_ds.at[i, r],
                recv_sem=r_ds.at[i, r], device_id={"tensor": t - 1}, device_id_type=MESH),
        )

    def product(d, r):
        return jnp.dot(tok[rows(r), :], w[d], preferred_element_type=F32)

    def encode(v, q_ref, s_ref, i, r):
        top = jnp.maximum(jnp.max(jnp.abs(v), axis=0, keepdims=True), 1e-30)
        q_ref[i, rows(r), :] = jnp.round(v * (LEVELS / top)).astype(jnp.int32).astype(jnp.int16)
        s_ref[i, r] = top * (1.0 / LEVELS)

    def decode(q_ref, s_ref, i, r):
        return q_ref[i, rows(r), :].astype(jnp.int32).astype(F32) * s_ref[i, r]

    def before_up(p, r):
        for c in u_copy(T - 2 - p, r):
            c.wait_send()

    def before_down(p, r):
        for c in d_copy(p, r):
            c.wait_send()

    def throttle(p, r, before):
        @pl.when(r >= AHEAD)
        def _():
            before(p, r - AHEAD)

        if p > 0:
            @pl.when(r < AHEAD)
            def _():
                before(p - 1, r + R - AHEAD)

    def phase(p):
        du, dd = T - 1 - p, p
        iu, idn = du - 1, dd

        def step(k, first):
            u, d = k - lag_u, k - lag_d
            up_on = (t < du) & (u >= 0) & (u < R)
            down_on = (t > dd) & (d >= 0) & (d < R)
            if first:
                tok_copy(0).wait()

                @pl.when(lower)
                def _():
                    w_copy(du).wait()

                @pl.when(upper)
                def _():
                    w_copy(dd).wait()

                load_rest()
            elif p == 0:
                @pl.when(k < R)
                def _():
                    tok_copy(k).wait()

            @pl.when(up_on)
            def _():
                acc[rows(u), :] = product(du, u)

                @pl.when(t == 0)
                def _():
                    encode(acc[rows(u), :], su, ssu, iu, u)

            @pl.when(down_on)
            def _():
                hold[...] = product(dd, d)

                @pl.when(t == T - 1)
                def _():
                    encode(hold[...], sd, ssd, idn, d)

            if first:
                pl.semaphore_wait(
                    bar, has_lo.astype(jnp.int32) + has_hi.astype(jnp.int32) + len(peers))
                gather_start()

            @pl.when(up_on)
            def _():
                @pl.when(has_lo)
                def _():
                    for c in u_copy(iu, u):
                        c.wait_recv()
                    encode(acc[rows(u), :] + decode(ru, rsu, iu, u), su, ssu, iu, u)

                throttle(p, u, before_up)
                for c in u_copy(iu, u):
                    c.start()

            @pl.when(down_on)
            def _():
                @pl.when(has_hi)
                def _():
                    for c in d_copy(idn, d):
                        c.wait_recv()
                    encode(hold[...] + decode(rd, rsd, idn, d), sd, ssd, idn, d)

                throttle(p, d, before_down)
                for c in d_copy(idn, d):
                    c.start()

            if p == T - 2:
                @pl.when((u == 0) & (t == 0))
                def _():
                    for c in low_up():
                        c.wait_send()

                @pl.when((d == 0) & (t == T - 1))
                def _():
                    for c in low_down():
                        c.wait_send()

            if first:
                @pl.when(lower & has_lo)
                def _():
                    w_copy(dd).wait()

                @pl.when(upper & has_hi)
                def _():
                    w_copy(du).wait()

            return 0

        if p == 0:
            step(0, True)
        lax.fori_loop(1 if p == 0 else 0, R + LAG, lambda k, _: step(k, False), 0)

    def low_start():
        own_dn.wait()
        own_up.wait()
        for s in range(X - 1):
            for k in range(2):
                x_copy(s, k).wait_recv()
            for k in range(2):
                if s < X - 2:
                    x_copy(s + 1, k).start()
                c_copy(s + 1, k).start()
        for s in range(X):
            for k in range(2):
                c_copy(s, k).wait_recv()

        def block(b, _):
            slot = slot_of[apb[pos * NB + b]]
            at = pl.ds(pl.multiple_of(b * BL, BL), BL)
            low[b] = lax.dot_general(
                dn[slot], tok[at, :], (((1,), (1,)), ((), ())), preferred_element_type=F32)
            return 0


        lax.fori_loop(0, NB, block, 0)

        @pl.when(t == 0)
        def _():
            low_send(low[...], lsu, slu, low_up())

        @pl.when(t == T - 1)
        def _():
            low_send(low[...], lsd, sld, low_down())

    def low_copies(src, dst, scale_src, scale_dst, at, target):
        return [
            pltpu.make_async_remote_copy(
                src_ref=a, dst_ref=b, send_sem=s_low.at[at, k], recv_sem=r_low.at[at, k],
                device_id={"tensor": target}, device_id_type=MESH)
            for k, (a, b) in enumerate([(src, dst), (scale_src, scale_dst)])
        ]

    def low_up():
        return low_copies(lsu, lru, slu, rlu, 0, t + 1)

    def low_down():
        return low_copies(lsd, lrd, sld, rld, 1, t - 1)

    def low_send(v, q_ref, s_ref, copies):
        top = jnp.maximum(jnp.max(jnp.abs(v), axis=1, keepdims=True), 1e-30)
        q_ref[...] = jnp.round(v * (LEVELS / top)).astype(jnp.int32).astype(jnp.int16)
        s_ref[...] = top * (1.0 / LEVELS)
        for c in copies:
            c.start()

    def low_decode(q_ref, s_ref):
        return q_ref[...].astype(jnp.int32).astype(F32) * s_ref[...]

    def low_finish():
        @pl.when(has_lo)
        def _():
            for c in low_up():
                c.wait_recv()

            @pl.when(has_hi)
            def _():
                low_send(low[...] + low_decode(lru, rlu), lsu, slu, low_up())

        @pl.when(has_hi)
        def _():
            for c in low_down():
                c.wait_recv()

            @pl.when(has_lo)
            def _():
                low_send(low[...] + low_decode(lrd, rld), lsd, sld, low_down())

            low[...] += low_decode(lrd, rld)

        @pl.when(has_lo)
        def _():
            low[...] += low_decode(lru, rlu)

    waited = {0, T - 1}
    for p in range(T - 1):
        for d in (T - 1 - p, p):
            if d not in waited:
                w_copy(d).wait()
                waited.add(d)
        if p == T - 2:
            low_start()
        phase(p)

    for d in (0, T - 1):
        @pl.when(t == d)
        def _():
            w_copy(d).wait()

    def own(r, _):
        acc[rows(r), :] = product(t, r)
        return 0

    lax.fori_loop(0, R, own, 0)
    low_finish()

    def lora(b, _):
        slot = slot_of[apb[pos * NB + b]]
        at = pl.ds(pl.multiple_of(b * BL, BL), BL)
        whole = low[b]
        first = whole.astype(jnp.bfloat16)
        rest = whole - first.astype(F32)
        second = rest.astype(jnp.bfloat16)
        third = (rest - second.astype(F32)).astype(jnp.bfloat16)
        factor = up[slot]
        term = lax.dot_general(
            jnp.concatenate([first, second, third], axis=0),
            jnp.concatenate([factor] * 3, axis=0),
            (((0,), (0,)), ((), ())), preferred_element_type=F32)
        acc[at, :] += ADAPTER_SCALE * term
        return 0

    lax.fori_loop(0, NB, lora, 0)

    def finish(r, _):
        @pl.when(has_hi)
        def _():
            for c in d_copy(t, r):
                c.wait_recv()
            acc[rows(r), :] += decode(rd, rsd, t, r)

        @pl.when(has_lo)
        def _():
            for c in u_copy(t - 1, r):
                c.wait_recv()
            acc[rows(r), :] += decode(ru, rsu, t - 1, r)

        for j in range(RB // BL):
            b = r * (RB // BL) + j
            at = pl.ds(pl.multiple_of(b * BL, BL), BL)
            here = lax.broadcasted_iota(jnp.int32, (BL, N), 0) < live[b]
            out[at, :] = jnp.where(here, acc[at, :], 0.0).astype(out.dtype)
        return 0

    lax.fori_loop(0, R, finish, 0)

    @pl.when(has_hi)
    def _():
        for j in range(AHEAD):
            for c in u_copy(t, R - AHEAD + j):
                c.wait_send()

    @pl.when(has_lo)
    def _():
        for j in range(AHEAD):
            for c in d_copy(t - 1, R - AHEAD + j):
                c.wait_send()

    @pl.when(has_lo & has_hi)
    def _():
        for c in low_up() + low_down():
            c.wait_send()

    for k in range(2):
        for s in range(X - 1):
            x_copy(s, k).wait_send()
        for s in range(X):
            c_copy(s, k).wait_send()


def on_device(T, DP, tokens, weight, down, up, apb, live, slot_of):
    X = DP // 2
    M, K = tokens.shape
    N = weight.shape[1] // T
    NB = live.shape[0]
    BL = M // NB
    AP, RANK = down.shape[0], down.shape[2]
    A = AP * DP
    R = max(1, min(4, NB))
    down = jnp.swapaxes(down, 1, 2)
    bf16, i16 = jnp.bfloat16, jnp.int16
    D = max(T - 1, 1)
    V, DMA = pltpu.VMEM, pltpu.SemaphoreType.DMA
    smem = pl.BlockSpec(memory_space=pltpu.SMEM)
    hbm = pl.BlockSpec(memory_space=pl.ANY)
    scratch = (
        [V((M, K), bf16), V((T, K, N), bf16), V((A, RANK, K), bf16), V((A, RANK, N), bf16)]
        + [V((M, N), F32), V((M // R, N), F32), V((NB, RANK, BL), F32)]
        + [V((D, M, N), i16)] * 4
        + [V((D, R, 1, N), F32)] * 4
        + [V((NB, RANK, BL), i16)] * 4
        + [V((NB, 1, BL), F32)] * 4
        + [DMA((R,)), DMA((T,)), DMA((2,))]
        + [DMA((D, R))] * 8
        + [DMA((2, 2)), DMA((2, 2))]
        + [DMA((max(X - 1, 1), 2)), DMA((max(X - 1, 1), 2)), DMA((X, 2)), DMA((X, 2))]
    )
    return pl.pallas_call(
        functools.partial(kernel, T, X, R, NB, BL),
        out_shape=jax.ShapeDtypeStruct((M, N), bf16),
        in_specs=[smem, smem, smem, hbm, hbm, hbm, hbm],
        out_specs=pl.BlockSpec(memory_space=pltpu.VMEM),
        scratch_shapes=scratch,
        compiler_params=pltpu.CompilerParams(
            collective_id=0, has_side_effects=True, vmem_limit_bytes=56 * 2**20),
        cost_estimate=pl.CostEstimate(
            flops=2 * M * K * N * T, bytes_accessed=2 * (M * K + K * N * T), transcendentals=0),
    )(apb, slot_of, live, tokens, weight, down, up)


def solution(mesh):
    placed = (
        P(("groups", "dp"), "tensor"),
        P("tensor", None),
        P(("groups", "dp"), "tensor", None),
        P(("groups", "dp"), None, "tensor"),
        P("groups"),
        P(("groups", "dp")),
        P("groups"),
    )
    return jax.shard_map(
        functools.partial(on_device, mesh.shape["tensor"], mesh.shape["dp"]),
        mesh=mesh,
        in_specs=placed,
        out_specs=P(("groups", "dp"), "tensor"),
        check_vma=False,
    )
```
